32 devices in a mesh: var: 4 (over y, core), tok: 8 (over z, x).
Axes of the slice: x: 2, y: 2, z: 4, core: 2. Of those that a mesh axis runs over, the one named last changes fastest.
Arguments:
- patches: bfloat16 [72, 4, 1024], P('var', None, 'tok'), may hold values from -6 to 6
- slot_var: int32 [72], replicated, may hold values from -1 to 47, as said below
- patch_weight: bfloat16 [48, 4, 1024], replicated, may hold values from -3 to 3
- var_embed: bfloat16 [48, 1024], replicated, may hold values from -6 to 6
- query: bfloat16 [1024], replicated, may hold values from -16 to 16
- key_weight: bfloat16 [1024, 1024], P('tok'), may hold values from -0.1875 to 0.1875
- value_weight: bfloat16 [1024, 1024], P('tok'), may hold values from -0.1875 to 0.1875
- out_weight: bfloat16 [1024, 1024], P('tok'), may hold values from -0.1875 to 0.1875
- cotangent: bfloat16 [1024, 1024], P(('tok', 'var')), may hold values from -6 to 6
Outputs:
- aggregated: bfloat16 [1024, 1024], P(('tok', 'var'))
- patch_grad: float32 [72, 4096], P('var', 'tok')
The draws below stay inside these ranges and needn't reach their ends.
Inputs may be any that keep to these rules, and one draw needn't show every extreme that they name: `slot_var`: slot 18 * i + j belongs to index i of var. Every variable id stands in exactly one slot; empty slots hold -1. The live slots of an index come first and hold consecutive ids, rising from index to index. Every index holds at least one and at most 18 live slots, and some index holds exactly 18.
All inputs are finite; a program needn't handle non-finite values.
Results may differ from the reference program's by a relative error of at most 0.011.
Values may be sent and summed in bfloat16 or wider, within the bound.
A program may use at most 128 MiB of HBM per device.

```python
import math
import jax
import jax.numpy as jnp
from jax import lax

V = 48
D = 1024
H = 16
HD = 64
VSLOT = 18
SLOTS = 72
TOKENS = 1024
N_VAR = 4


def draw_slot_var(key, part):
    base = V // N_VAR
    extra = VSLOT - base
    order = jax.random.permutation(jax.random.fold_in(key, 11), N_VAR)
    shifts = jax.random.randint(jax.random.fold_in(key, 12), (N_VAR // 2,), 0, extra + 1).astype(jnp.int32)
    shifts = shifts.at[0].set(extra)
    deltas = jnp.concatenate([shifts, -shifts])
    counts = jnp.zeros((N_VAR,), jnp.int32).at[order].set(base + deltas)
    starts = jnp.cumsum(counts) - counts
    slots = jnp.arange(N_VAR * VSLOT, dtype=jnp.int32)
    owner = slots // VSLOT
    within = slots % VSLOT
    return jnp.where(within < counts[owner], starts[owner] + within, -1).astype(jnp.int32)


def block_scale(own_key, shape, cuts, smallest, top_value):
    def one(axis_at, blocks):
        heights = jax.random.uniform(jax.random.fold_in(jax.random.fold_in(own_key, 6), axis_at), (blocks,), jnp.float32, smallest / len(cuts), top_value / len(cuts))
        return jnp.repeat(jnp.exp(heights), shape[axis_at] // blocks).reshape((-1,) + (1,) * (len(shape) - axis_at - 1))

    loudness = one(*cuts[0])
    for cut in cuts[1:]:
        loudness = loudness * one(*cut)
    return loudness


def normal_values(key, dims, scale, most, shards=(), kind=jnp.bfloat16):
    result = jax.random.normal(key, dims, jnp.float32) * scale
    if len(shards) > 0:
        result = block_scale(key, dims, shards, -0.22, 0.18) * result
    return jnp.clip(result, min=-most, max=most).astype(kind)


def setup_inputs(seed: int = 0) -> dict:
    key_of = jax.random.split(jax.random.key(seed), 10)
    return {
        "patches": normal_values(key_of[0], (SLOTS, 4, TOKENS), 1.0, 6.0, ((0, 4), (2, 8))),
        "slot_var": draw_slot_var(jax.random.fold_in(key_of[9], 71), 0),
        "patch_weight": normal_values(key_of[2], (V, 4, D), 4 ** -0.5, 3.0),
        "var_embed": normal_values(key_of[3], (V, D), 1.0, 6.0),
        "query": normal_values(key_of[4], (D,), 4.0, 16.0),
        "key_weight": normal_values(key_of[5], (D, D), D ** -0.5, 0.1875, ((0, 8),)),
        "value_weight": normal_values(key_of[6], (D, D), D ** -0.5, 0.1875, ((0, 8),)),
        "out_weight": normal_values(key_of[7], (D, D), D ** -0.5, 0.1875, ((0, 8),)),
        "cotangent": normal_values(key_of[8], (TOKENS, D), 1.0, 6.0, ((0, 32),)),
    }


score_cap = 5.0
inv_sqrt_two = 1.0 / math.sqrt(2.0)
inv_sqrt_two_pi = 1.0 / math.sqrt(2.0 * math.pi)

def gelu_exact(inputs):
    return 0.5 * inputs * (1.0 + lax.erf(inputs * inv_sqrt_two))

def gelu_slope(inputs):
    return 0.5 * (1.0 + lax.erf(inputs * inv_sqrt_two)) + inputs * jnp.exp(-0.5 * inputs * inputs) * inv_sqrt_two_pi

def live_index(slot_var):
    ids = jnp.arange(V, dtype=jnp.int32)
    places = jnp.arange(slot_var.shape[0], dtype=jnp.int32)
    match = slot_var[None, :] == ids[:, None]
    return lax.optimization_barrier(jnp.sum(jnp.where(match, places[None, :], 0), axis=1)).astype(jnp.int32)

def attend(embedded, query, key_weight, value_weight, out_weight, cot_rows):
    var_count, tok_count, width = embedded.shape
    flat_rows = embedded.reshape(var_count * tok_count, width)
    key_heads = jnp.dot(flat_rows, key_weight, preferred_element_type=jnp.float32).astype(jnp.bfloat16).reshape(var_count, tok_count, H, HD)
    value_heads = jnp.dot(flat_rows, value_weight, preferred_element_type=jnp.float32).astype(jnp.bfloat16).reshape(var_count, tok_count, H, HD)
    query_heads = query.reshape(H, HD).astype(jnp.float32)
    raw_scores = jnp.einsum('vthj,hj->tvh', key_heads.astype(jnp.float32), query_heads) / math.sqrt(HD)
    squashed = jnp.tanh(raw_scores / score_cap)
    exp_scores = jnp.exp(score_cap * squashed)
    attn_f32 = exp_scores / lax.optimization_barrier(jnp.sum(exp_scores, axis=1, keepdims=True))
    attn_bf = attn_f32.astype(jnp.bfloat16)
    pooled = jnp.einsum('tvh,vthj->thj', attn_bf.astype(jnp.float32), value_heads.astype(jnp.float32)).astype(jnp.bfloat16).reshape(tok_count, width)
    mixed = jnp.dot(pooled, out_weight, preferred_element_type=jnp.float32).astype(jnp.bfloat16)
    grad_pooled = jnp.dot(cot_rows, out_weight.T, preferred_element_type=jnp.float32).astype(jnp.bfloat16).reshape(tok_count, H, HD)
    grad_attn = jnp.einsum('thj,vthj->tvh', grad_pooled.astype(jnp.float32), value_heads.astype(jnp.float32))
    attn_vth = jnp.transpose(attn_bf, (1, 0, 2)).astype(jnp.float32)
    grad_values = (attn_vth[:, :, :, None] * grad_pooled.astype(jnp.float32)[None]).astype(jnp.bfloat16)
    grad_scores = attn_f32 * (grad_attn - lax.optimization_barrier(jnp.sum(attn_f32 * grad_attn, axis=1, keepdims=True)))
    grad_raw = grad_scores * (1.0 - squashed * squashed) / math.sqrt(HD)
    grad_keys = (jnp.transpose(grad_raw, (1, 0, 2))[:, :, :, None] * query_heads[None, None]).astype(jnp.bfloat16)
    grad_embed = jnp.dot(grad_keys.reshape(var_count * tok_count, width), key_weight.T, preferred_element_type=jnp.float32)
    grad_embed = grad_embed + jnp.dot(grad_values.reshape(var_count * tok_count, width), value_weight.T, preferred_element_type=jnp.float32)
    return (mixed, grad_embed.astype(jnp.bfloat16).reshape(var_count, tok_count, width))

def reference(patches, slot_var, patch_weight, var_embed, query, key_weight, value_weight, out_weight, cotangent):
    live_slot = live_index(slot_var)
    live_pixels = jnp.take(patches, live_slot, axis=0)
    block = math.gcd(TOKENS, 256)
    count = TOKENS // block
    embed_f32 = var_embed.astype(jnp.float32)

    def one_block(carry, index):
        first_tok = (index * block).astype(jnp.int32)
        block_pixels = lax.dynamic_slice_in_dim(live_pixels, first_tok, block, 2)
        cot_rows = lax.dynamic_slice_in_dim(cotangent, first_tok, block, 0)
        pre_act = jnp.einsum('vpt,vpd->vtd', block_pixels, patch_weight, preferred_element_type=jnp.float32) + embed_f32[:, None, :]
        embedded = gelu_exact(pre_act).astype(jnp.bfloat16)
        mixed, grad_embed = attend(embedded, query, key_weight, value_weight, out_weight, cot_rows)
        grad_pre = grad_embed.astype(jnp.float32) * gelu_slope(pre_act)
        carry = carry + jnp.einsum('vpt,vtd->vpd', block_pixels.astype(jnp.float32), grad_pre, precision=lax.Precision.HIGHEST)
        return (carry, mixed)
    total, mixed_all = lax.scan(one_block, jnp.zeros((V, 4, D), jnp.float32), jnp.arange(count, dtype=jnp.int32))
    aggregated = mixed_all.reshape(TOKENS, D)
    patch_grad = jnp.zeros((SLOTS, 4 * D), jnp.float32).at[live_slot].set(total.reshape(V, 4 * D))
    return (aggregated, patch_grad)
```

```python
import functools
import math

import jax
import jax.numpy as jnp
from jax import lax
from jax.experimental import pallas as pl
from jax.experimental.pallas import tpu as pltpu
from jax.sharding import PartitionSpec as P

H = 16
HD = 64

score_cap = 5.0
inv_sqrt_two = 1.0 / math.sqrt(2.0)
inv_sqrt_two_pi = 1.0 / math.sqrt(2.0 * math.pi)

BF = jnp.bfloat16
F32 = jnp.float32
NT = (((1,), (1,)), ((), ()))
TN = (((0,), (0,)), ((), ()))


def main_kernel(
    n_tok,
    n_var,
    pix_ref,
    pw_ref,
    ve_ref,
    wq_ref,
    v_ref,
    o_ref,
    cot_ref,
    sel_ref,
    agg_ref,
    pg_ref,
    e_ref,
    slope_ref,
    g_ref,
    s_ref,
    lhs_ref,
    pe_ref,
    acc_ref,
):
    toks = cot_ref.shape[0]
    width = cot_ref.shape[1]
    lanes = 128
    spans = width // lanes
    tall = H * toks

    def token_rows(ref, t):
        cells = [ref[pl.ds(c * tall + t, H, stride=toks), :] for c in range(spans)]
        return jnp.concatenate(cells, axis=1)

    @pl.loop(0, toks)
    def _(t):
        pix = pix_ref[t]
        pre = ve_ref[...]
        for p in range(4):
            pre = pre + pix[:, p : p + 1] * pw_ref[p]
        cdf = 0.5 * (1.0 + lax.erf(pre * inv_sqrt_two))
        e_ref[t] = (pre * cdf).astype(BF)
        slope_ref[t] = cdf + pre * jnp.exp(-0.5 * pre * pre) * inv_sqrt_two_pi

    gp = lax.dot_general(cot_ref[...], o_ref[...], NT, preferred_element_type=F32)
    low = lax.broadcasted_iota(jnp.int32, (toks, 2 * HD), 1) < HD
    for pair in range(H // 2):
        cols = pl.ds(pair * 2 * HD, 2 * HD)
        part = gp[:, pair * 2 * HD : (pair + 1) * 2 * HD]
        both = jnp.concatenate([jnp.where(low, part, 0.0), jnp.where(low, 0.0, part)], axis=0)
        wide = lax.dot_general(both.astype(BF), v_ref[:, cols], NT, preferred_element_type=F32)
        for c in range(spans):
            rows = pl.ds(c * tall + pair * 2 * toks, 2 * toks)
            g_ref[rows, :] = wide[:, c * lanes : (c + 1) * lanes]

    wq = wq_ref[...]
    wq_hi = wq.astype(BF)
    wq_lo = (wq - wq_hi.astype(F32)).astype(BF)

    @pl.loop(0, toks)
    def _(t):
        g_t = token_rows(g_ref, t).astype(BF)
        rhs = jnp.concatenate([wq_hi, wq_lo, g_t], axis=0)
        s_ref[t] = lax.dot_general(e_ref[t], rhs, NT, preferred_element_type=F32)

    s = s_ref[...]
    raw = (s[:, :, :H] + s[:, :, H : 2 * H]) * (1.0 / math.sqrt(HD))
    grad_attn = s[:, :, 2 * H :]
    squashed = jnp.tanh(raw * (1.0 / score_cap))
    exp_scores = jnp.exp(score_cap * squashed)
    attn = exp_scores / jnp.sum(exp_scores, axis=1, keepdims=True)
    grad_scores = attn * (grad_attn - jnp.sum(attn * grad_attn, axis=1, keepdims=True))
    grad_raw = grad_scores * (1.0 - squashed * squashed) * (1.0 / math.sqrt(HD))
    lhs_ref[...] = jnp.concatenate([attn, grad_raw], axis=2).astype(BF)

    acc_ref[...] = jnp.zeros_like(acc_ref)

    @pl.loop(0, toks)
    def _(t):
        g_t = token_rows(g_ref, t).astype(BF)
        lhs = lhs_ref[t]
        mixed = lax.dot_general(lhs[:, :H], e_ref[t], TN, preferred_element_type=F32)
        for c in range(spans):
            cell = mixed[:, c * lanes : (c + 1) * lanes]
            pe_ref[pl.ds(c * tall + t, H, stride=toks), :] = cell
        rhs = jnp.concatenate([g_t, wq_hi], axis=0)
        grad_pre = jnp.dot(lhs, rhs, preferred_element_type=F32) * slope_ref[t]
        pix = pix_ref[t]
        for p in range(4):
            acc_ref[p] += pix[:, p : p + 1] * grad_pre

    cut = 4 * width // n_tok
    for p in range(4):
        part = acc_ref[p].astype(BF)
        for i in range(n_var):
            rows = jnp.dot(sel_ref[i], part, preferred_element_type=F32).astype(BF)
            for c in range(width // cut):
                k = p * (width // cut) + c
                pg_ref[k * n_var + i] = rows[:, c * cut : (c + 1) * cut]

    pieces = []
    for pair in range(H // 2):
        both = jnp.concatenate(
            [pe_ref[pl.ds(c * tall + pair * 2 * toks, 2 * toks), :] for c in range(spans)],
            axis=1,
        ).astype(BF)
        cols = pl.ds(pair * 2 * HD, 2 * HD)
        two = jnp.dot(both, v_ref[:, cols], preferred_element_type=F32)
        pieces.append(jnp.where(low, two[:toks], two[toks:]))
    pooled = jnp.concatenate(pieces, axis=1).astype(BF)
    agg_ref[...] = jnp.dot(pooled, o_ref[...], preferred_element_type=F32).astype(BF)


def compute(n_tok, n_var, pix, pw, ve, wq, v, o, cot, sel):
    toks, width = cot.shape
    vars_ = ve.shape[0]
    local_slots = sel.shape[1]
    vm = pl.BlockSpec(memory_space=pltpu.VMEM)
    return pl.pallas_call(
        functools.partial(main_kernel, n_tok, n_var),
        out_shape=(
            jax.ShapeDtypeStruct((toks, width), BF),
            jax.ShapeDtypeStruct((n_tok * n_var, local_slots, 4 * width // n_tok), BF),
        ),
        in_specs=[vm] * 8,
        out_specs=(vm, vm),
        scratch_shapes=[
            pltpu.VMEM((toks, vars_, width), BF),
            pltpu.VMEM((toks, vars_, width), F32),
            pltpu.VMEM((width // 128 * H * toks, 128), F32),
            pltpu.VMEM((toks, vars_, 3 * H), F32),
            pltpu.VMEM((toks, vars_, 2 * H), BF),
            pltpu.VMEM((width // 128 * H * toks, 128), F32),
            pltpu.VMEM((4, vars_, width), F32),
        ],
        compiler_params=pltpu.CompilerParams(vmem_limit_bytes=56 * 1024 * 1024),
    )(pix, pw, ve, wq, v, o, cot, sel)


def body(
    n_tok,
    n_var,
    patches,
    slot_var,
    patch_weight,
    var_embed,
    query,
    key_weight,
    value_weight,
    out_weight,
    cotangent,
):
    var_total, _, width = patch_weight.shape
    local_slots = patches.shape[0]
    toks = cotangent.shape[0]
    wq_rows = jnp.einsum(
        "dhj,hj->hd",
        key_weight.reshape(-1, H, HD).astype(F32),
        query.reshape(H, HD).astype(F32),
        precision=lax.Precision.HIGHEST,
    )
    mine = patches.reshape(local_slots, 4, n_var, toks).transpose(2, 0, 1, 3)
    pixels = lax.all_to_all(mine, "var", split_axis=0, concat_axis=0, tiled=True)
    pixels = pixels.reshape(n_var * local_slots, 4 * toks)
    wq = lax.all_gather(wq_rows, "tok", axis=1, tiled=True)
    o = lax.all_gather(out_weight, "tok", axis=0, tiled=True)
    v = lax.all_gather(value_weight, "tok", axis=0, tiled=True)
    picker = slot_var[:, None] == jnp.arange(var_total, dtype=jnp.int32)[None, :]
    picker = picker.astype(BF)
    live = lax.dot_general(picker, pixels, TN, preferred_element_type=F32)
    pix = live.reshape(var_total, 4, toks).transpose(2, 0, 1)
    pw = patch_weight.transpose(1, 0, 2).astype(F32)
    agg, blocks = compute(
        n_tok,
        n_var,
        pix,
        pw,
        var_embed.astype(F32),
        wq,
        v,
        o,
        cotangent,
        picker.reshape(n_var, local_slots, var_total),
    )
    got = lax.all_to_all(blocks, ("tok", "var"), split_axis=0, concat_axis=0, tiled=True)
    return agg, jnp.sum(got.astype(F32), axis=0)


def solution(mesh):
    return jax.shard_map(
        functools.partial(body, mesh.shape["tok"], mesh.shape["var"]),
        mesh=mesh,
        in_specs=(
            P("var", None, "tok"),
            P(),
            P(),
            P(),
            P(),
            P("tok", None),
            P("tok", None),
            P("tok", None),
            P(("tok", "var"), None),
        ),
        out_specs=(P(("tok", "var"), None), P("var", "tok")),
        check_vma=False,
    )
```

```python
import functools
import math

import jax
import jax.numpy as jnp
from jax import lax
from jax.experimental import pallas as pl
from jax.experimental.pallas import tpu as pltpu
from jax.sharding import PartitionSpec as P

H = 16
HD = 64

score_cap = 5.0
inv_sqrt_two = 1.0 / math.sqrt(2.0)
inv_sqrt_two_pi = 1.0 / math.sqrt(2.0 * math.pi)

BF = jnp.bfloat16
F32 = jnp.float32
NT = (((1,), (1,)), ((), ()))
TN = (((0,), (0,)), ((), ()))


def all_kernel(
    n_tok,
    n_var,
    pat_ref,
    wqs_ref,
    wsh_ref,
    pw_ref,
    ve_ref,
    cot_ref,
    sel_ref,
    spread_ref,
    agg_ref,
    sum_ref,
    pixels_ref,
    wqa_ref,
    w_ref,
    pix_ref,
    e_ref,
    slope_ref,
    g_ref,
    s_ref,
    lhs_ref,
    pe_ref,
    acc_ref,
    out_ref,
    in_ref,
    pat_send,
    pat_recv,
    wq_send,
    wq_recv,
    tok_send,
    tok_recv,
    row_send,
    row_recv,
    sib_send,
    sib_recv,
    sum_send,
    sum_recv,
):
    toks, width = cot_ref.shape
    rows = wsh_ref.shape[0]
    lanes = 128
    spans = width // lanes
    tall = H * toks
    total = n_tok * n_var
    wide = 2 * width // n_var
    pairs = n_var // 2
    block = 256
    me_t = lax.axis_index("tok")
    me_v = lax.axis_index("var")
    me = me_t * n_var + me_v
    sibling = me_v + 1 - 2 * lax.rem(me_v, 2)

    def remote(src, dst, send, recv, **place):
        return pltpu.make_async_remote_copy(
            src_ref=src,
            dst_ref=dst,
            send_sem=send,
            recv_sem=recv,
            device_id=place,
            device_id_type=pl.DeviceIdType.MESH,
        )

    def peer(n):
        at = lax.rem(me + n, total)
        return {"tok": at // n_var, "var": lax.rem(at, n_var)}

    barrier = pltpu.get_barrier_semaphore()

    @pl.loop(1, total)
    def _(n):
        pl.semaphore_signal(
            barrier, inc=1, device_id=peer(n), device_id_type=pl.DeviceIdType.MESH
        )

    pl.semaphore_wait(barrier, total - 1)

    pat_copies = []
    for n in range(1, n_var):
        to = lax.rem(me_v + n, n_var)
        copy = remote(
            pat_ref.at[to], pixels_ref.at[me_v], pat_send.at[n], pat_recv.at[n], var=to
        )
        copy.start()
        pat_copies.append(copy)
    wq_copies = []
    tok_copies = []
    for n in range(1, n_tok):
        to = lax.rem(me_t + n, n_tok)
        spot = (
            pl.ds(pl.multiple_of(me_t * rows, rows), rows),
            pl.ds(pl.multiple_of(me_v * wide, wide), wide),
        )
        copy = remote(wsh_ref.at[:, spot[1]], w_ref.at[spot], tok_send.at[n], tok_recv.at[n], tok=to)
        copy.start()
        tok_copies.append(copy)
        copy = remote(wqs_ref, wqa_ref.at[me_t], wq_send.at[n], wq_recv.at[n], tok=to)
        copy.start()
        wq_copies.append(copy)

    pixels_ref[me_v] = pat_ref[me_v]
    wqa_ref[me_t] = wqs_ref[...]
    w_ref[pl.ds(pl.multiple_of(me_t * rows, rows), rows), :] = wsh_ref[...]
    acc_ref[...] = jnp.zeros_like(acc_ref)

    row_copies = []
    sib_copies = []

    def to_sibling(n, m, spot):
        at = (n - 1) * pairs + m
        copy = remote(w_ref.at[spot], w_ref.at[spot], sib_send.at[at], sib_recv.at[at], var=sibling)
        copy.start()
        sib_copies.append(copy)

    def place_of(n, m):
        source = lax.rem(me_t + n_tok - n, n_tok)
        owner = lax.rem(me_v + n_var - 2 * m, n_var)
        return (
            pl.ds(pl.multiple_of(source * rows, rows), rows),
            pl.ds(pl.multiple_of(owner * wide, wide), wide),
        )

    def pass_first(n):
        tok_copies[n - 1].wait_recv()
        spot = place_of(n, 0)
        for m in range(1, pairs):
            at = (n - 1) * (pairs - 1) + m - 1
            to = lax.rem(me_v + 2 * m, n_var)
            copy = remote(w_ref.at[spot], w_ref.at[spot], row_send.at[at], row_recv.at[at], var=to)
            copy.start()
            row_copies.append(copy)
        to_sibling(n, 0, spot)

    def pass_second(n):
        for m in range(1, pairs):
            row_copies[(n - 1) * (pairs - 1) + m - 1].wait_recv()
            to_sibling(n, m, place_of(n, m))

    for copy in pat_copies:
        copy.wait_recv()
    live = lax.dot_general(sel_ref[0], pixels_ref[0], TN, preferred_element_type=F32)
    for i in range(1, n_var):
        live += lax.dot_general(sel_ref[i], pixels_ref[i], TN, preferred_element_type=F32)
    lane_at = lax.broadcasted_iota(jnp.int32, live.shape, 1)

    def embed(first, count):
        @pl.loop(first, first + count)
        def _(t):
            cols = []
            for p in range(4):
                col = jnp.sum(
                    jnp.where(lane_at == p * toks + t, live, 0.0), axis=1, keepdims=True
                )
                pix_ref[t, :, p : p + 1] = col
                cols.append(col)
            for c in range(0, width, block):
                span = slice(c, c + block)
                pre = ve_ref[:, span]
                for p in range(4):
                    pre = pre + cols[p] * pw_ref[p, :, span]
                cdf = 0.5 * (1.0 + lax.erf(pre * inv_sqrt_two))
                e_ref[t, :, span] = (pre * cdf).astype(BF)
                slope_ref[t, :, span] = cdf + pre * jnp.exp(-0.5 * pre * pre) * inv_sqrt_two_pi

    steps = 8
    first_done, second_done = 1, 1
    for c in range(steps):
        embed(c * (toks // steps), toks // steps)
        upto = 1 + (c + 1) * (n_tok - 1) // steps
        while second_done < first_done:
            pass_second(second_done)
            second_done += 1
        while first_done < upto:
            pass_first(first_done)
            first_done += 1
    while second_done < first_done:
        pass_second(second_done)
        second_done += 1

    for copy in wq_copies:
        copy.wait_recv()
    for copy in sib_copies:
        copy.wait_recv()

    gp = lax.dot_general(cot_ref[...], w_ref[:, width:], NT, preferred_element_type=F32)
    low = lax.broadcasted_iota(jnp.int32, (toks, 2 * HD), 1) < HD
    for pair in range(H // 2):
        part = gp[:, pair * 2 * HD : (pair + 1) * 2 * HD]
        both = jnp.concatenate([jnp.where(low, part, 0.0), jnp.where(low, 0.0, part)], axis=0)
        carried = lax.dot_general(
            both.astype(BF),
            w_ref[:, pair * 2 * HD : (pair + 1) * 2 * HD],
            NT,
            preferred_element_type=F32,
        )
        for c in range(spans):
            g_ref[pl.ds(c * tall + pair * 2 * toks, 2 * toks), :] = carried[
                :, c * lanes : (c + 1) * lanes
            ]

    def token_rows(t):
        cells = [g_ref[pl.ds(c * tall + t, H, stride=toks), :] for c in range(spans)]
        return jnp.concatenate(cells, axis=1).astype(BF)

    wq = jnp.concatenate([wqa_ref[k] for k in range(n_tok)], axis=1)
    wq_hi = wq.astype(BF)
    wq_lo = (wq - wq_hi.astype(F32)).astype(BF)
    group = 4

    @pl.loop(0, toks // group)
    def _(step):
        for u in range(group):
            t = step * group + u
            rhs = jnp.concatenate([wq_hi, wq_lo, token_rows(t)], axis=0)
            s_ref[t] = lax.dot_general(e_ref[t], rhs, NT, preferred_element_type=F32)

    s = s_ref[...]
    raw = (s[:, :, :H] + s[:, :, H : 2 * H]) * (1.0 / math.sqrt(HD))
    grad_attn = s[:, :, 2 * H :]
    squashed = jnp.tanh(raw * (1.0 / score_cap))
    exp_scores = jnp.exp(score_cap * squashed)
    attn = exp_scores / jnp.sum(exp_scores, axis=1, keepdims=True)
    grad_scores = attn * (grad_attn - jnp.sum(attn * grad_attn, axis=1, keepdims=True))
    grad_raw = grad_scores * (1.0 - squashed * squashed) * (1.0 / math.sqrt(HD))
    lhs_ref[...] = jnp.concatenate([attn, grad_raw], axis=2).astype(BF)

    @pl.loop(0, toks // group)
    def _(step):
        cols, left, right = [], [], []
        for u in range(group):
            t = step * group + u
            lhs = lhs_ref[t]
            mixed = lax.dot_general(lhs[:, :H], e_ref[t], TN, preferred_element_type=F32)
            for c in range(spans):
                cell = mixed[:, c * lanes : (c + 1) * lanes]
                pe_ref[pl.ds(c * tall + t, H, stride=toks), :] = cell
            left.append(lhs)
            right.append(jnp.concatenate([token_rows(t), wq_hi], axis=0))
            pix = pix_ref[t]
            cols.append([pix[:, p : p + 1] for p in range(4)])
        for c in range(0, width, block):
            span = slice(c, c + block)
            grads = [
                jnp.dot(left[u], right[u][:, span], preferred_element_type=F32)
                * slope_ref[step * group + u, :, span]
                for u in range(group)
            ]
            for p in range(4):
                more = cols[0][p] * grads[0]
                for u in range(1, group):
                    more = more + cols[u][p] * grads[u]
                acc_ref[p, :, span] += more

    cut = 4 * width // n_tok
    chunks = cut // lanes
    tall_out = in_ref.shape[1]
    for k in range(n_tok):
        p, start = k * cut // width, k * cut % width
        stacked = jnp.concatenate(
            [
                acc_ref[p, :, start + c * lanes : start + (c + 1) * lanes].astype(BF)
                for c in range(chunks)
            ],
            axis=0,
        )
        placed = jnp.dot(spread_ref[...], stacked, preferred_element_type=F32).astype(BF)
        for i in range(n_var):
            out_ref[k * n_var + i] = placed[i * tall_out : (i + 1) * tall_out]

    @pl.loop(1, total)
    def _(n):
        to = peer(n)
        at = to["tok"] * n_var + to["var"]
        remote(out_ref.at[at], in_ref.at[n], sum_send.at[n], sum_recv.at[n], **to).start()

    pieces = []
    for pair in range(H // 2):
        both = jnp.concatenate(
            [pe_ref[pl.ds(c * tall + pair * 2 * toks, 2 * toks), :] for c in range(spans)],
            axis=1,
        ).astype(BF)
        two = jnp.dot(
            both, w_ref[:, pair * 2 * HD : (pair + 1) * 2 * HD], preferred_element_type=F32
        )
        pieces.append(jnp.where(low, two[:toks], two[toks:]))
    pooled = jnp.concatenate(pieces, axis=1).astype(BF)
    agg_ref[...] = jnp.dot(pooled, w_ref[:, width:], preferred_element_type=F32).astype(BF)

    sum_ref[...] = out_ref[me].astype(F32)

    @pl.loop(1, total)
    def _(n):
        to = peer(n)
        at = to["tok"] * n_var + to["var"]
        copy = remote(out_ref.at[at], in_ref.at[n], sum_send.at[n], sum_recv.at[n], **to)
        copy.wait()
        sum_ref[...] += in_ref[n].astype(F32)

    for copy in pat_copies + wq_copies + tok_copies + row_copies + sib_copies:
        copy.wait_send()


def compute(n_tok, n_var, pat, wqs, wsh, pw, ve, cot, sel, spread):
    toks, width = cot.shape
    vars_ = ve.shape[0]
    rows = wsh.shape[0]
    pairs = n_var // 2
    total = n_tok * n_var
    tall_out = spread.shape[0] // n_var
    vm = pl.BlockSpec(memory_space=pltpu.VMEM)
    dma = pltpu.SemaphoreType.DMA
    return pl.pallas_call(
        functools.partial(all_kernel, n_tok, n_var),
        out_shape=(
            jax.ShapeDtypeStruct((toks, width), BF),
            jax.ShapeDtypeStruct((tall_out, 128), F32),
        ),
        in_specs=[vm] * 8,
        out_specs=(vm, vm),
        scratch_shapes=[
            pltpu.VMEM(pat.shape, BF),
            pltpu.VMEM((n_tok,) + wqs.shape, F32),
            pltpu.VMEM((width, 2 * width), BF),
            pltpu.VMEM((toks, vars_, 4), F32),
            pltpu.VMEM((toks, vars_, width), BF),
            pltpu.VMEM((toks, vars_, width), F32),
            pltpu.VMEM((width // 128 * H * toks, 128), F32),
            pltpu.VMEM((toks, vars_, 3 * H), F32),
            pltpu.VMEM((toks, vars_, 2 * H), BF),
            pltpu.VMEM((width // 128 * H * toks, 128), F32),
            pltpu.VMEM((4, vars_, width), F32),
            pltpu.VMEM((total, tall_out, 128), BF),
            pltpu.VMEM((total, tall_out, 128), BF),
            dma((n_var,)),
            dma((n_var,)),
            dma((n_tok,)),
            dma((n_tok,)),
            dma((n_tok,)),
            dma((n_tok,)),
            dma((n_tok * pairs,)),
            dma((n_tok * pairs,)),
            dma((n_tok * pairs,)),
            dma((n_tok * pairs,)),
            dma((total,)),
            dma((total,)),
        ],
        compiler_params=pltpu.CompilerParams(
            vmem_limit_bytes=56 * 1024 * 1024, collective_id=0, has_side_effects=True
        ),
    )(pat, wqs, wsh, pw, ve, cot, sel, spread)


def body(
    n_tok,
    n_var,
    patches,
    slot_var,
    patch_weight,
    var_embed,
    query,
    key_weight,
    value_weight,
    out_weight,
    cotangent,
):
    var_total, _, width = patch_weight.shape
    local_slots = patches.shape[0]
    toks = cotangent.shape[0]
    wq_rows = jnp.einsum(
        "dhj,hj->hd",
        key_weight.reshape(-1, H, HD).astype(F32),
        query.reshape(H, HD).astype(F32),
        precision=lax.Precision.HIGHEST,
    )
    pad = -local_slots % 16
    mine = patches.reshape(local_slots, 4, n_var, toks).transpose(2, 0, 1, 3)
    mine = mine.reshape(n_var, local_slots, 4 * toks)
    mine = jnp.pad(mine, ((0, 0), (0, pad), (0, 0)))
    picker = slot_var[:, None] == jnp.arange(var_total, dtype=jnp.int32)[None, :]
    picker = picker.astype(BF).reshape(n_var, local_slots, var_total)
    chunks = 4 * width // n_tok // 128
    spread = jnp.einsum("isv,cb->icsbv", picker, jnp.eye(chunks, dtype=BF))
    spread = spread.reshape(n_var, chunks * local_slots, chunks * var_total)
    spread = jnp.pad(spread, ((0, 0), (0, -(chunks * local_slots) % 16), (0, 0)))
    agg, sums = compute(
        n_tok,
        n_var,
        mine,
        wq_rows,
        jnp.concatenate([value_weight, out_weight], axis=1),
        patch_weight.transpose(1, 0, 2).astype(F32),
        var_embed.astype(F32),
        cotangent,
        jnp.pad(picker, ((0, 0), (0, pad), (0, 0))),
        spread.reshape(-1, chunks * var_total),
    )
    sums = sums[: chunks * local_slots].reshape(chunks, local_slots, 128)
    return agg, sums.transpose(1, 0, 2).reshape(local_slots, chunks * 128)


def solution(mesh):
    return jax.shard_map(
        functools.partial(body, mesh.shape["tok"], mesh.shape["var"]),
        mesh=mesh,
        in_specs=(
            P("var", None, "tok"),
            P(),
            P(),
            P(),
            P(),
            P("tok", None),
            P("tok", None),
            P("tok", None),
            P(("tok", "var"), None),
        ),
        out_specs=(P(("tok", "var"), None), P("var", "tok")),
        check_vma=False,
    )
```

```python
import functools
import math

import jax
import jax.numpy as jnp
from jax import lax
from jax.experimental import pallas as pl
from jax.experimental.pallas import tpu as pltpu
from jax.sharding import PartitionSpec as P

H = 16
HD = 64

score_cap = 5.0
inv_sqrt_two = 1.0 / math.sqrt(2.0)
inv_sqrt_two_pi = 1.0 / math.sqrt(2.0 * math.pi)

BF = jnp.bfloat16
F32 = jnp.float32
NT = (((1,), (1,)), ((), ()))
TN = (((0,), (0,)), ((), ()))


def all_kernel(
    n_tok,
    n_var,
    pat_ref,
    slot_ref,
    query_ref,
    kw_ref,
    vw_ref,
    ow_ref,
    pw_ref,
    ve_ref,
    cot_ref,
    agg_ref,
    sum_ref,
    total_ref,
    pixels_ref,
    wqs_ref,
    wqa_ref,
    w_ref,
    pix_ref,
    e_ref,
    slope_ref,
    g_ref,
    attn_ref,
    slope_s_ref,
    s_ref,
    lhs_ref,
    pe_ref,
    acc_ref,
    out_ref,
    in_ref,
    pat_send,
    pat_recv,
    wq_send,
    wq_recv,
    tok_send,
    tok_recv,
    row_send,
    row_recv,
    sib_send,
    sib_recv,
    sum_send,
    sum_recv,
):
    toks, width = cot_ref.shape
    rows = vw_ref.shape[0]
    vars_ = ve_ref.shape[0]
    slots = slot_ref.shape[1]
    local_slots = slots // n_var
    lanes = 128
    spans = width // lanes
    tall = H * toks
    total = n_tok * n_var
    wide = 2 * width // n_var
    pairs = n_var // 2
    block = 256
    me_t = lax.axis_index("tok")
    me_v = lax.axis_index("var")
    me = me_t * n_var + me_v
    sibling = me_v + 1 - 2 * lax.rem(me_v, 2)

    def remote(src, dst, send, recv, **place):
        return pltpu.make_async_remote_copy(
            src_ref=src,
            dst_ref=dst,
            send_sem=send,
            recv_sem=recv,
            device_id=place,
            device_id_type=pl.DeviceIdType.MESH,
        )

    def peer(n):
        at = lax.rem(me + n, total)
        return {"tok": at // n_var, "var": lax.rem(at, n_var)}

    barrier = pltpu.get_barrier_semaphore()

    @pl.loop(1, total)
    def _(n):
        pl.semaphore_signal(
            barrier, inc=1, device_id=peer(n), device_id_type=pl.DeviceIdType.MESH
        )

    pl.semaphore_wait(barrier, total - 1)

    pat_copies = []
    for n in range(1, n_var):
        to = lax.rem(me_v + n, n_var)
        copy = remote(
            pat_ref.at[to], pixels_ref.at[me_v], pat_send.at[n], pat_recv.at[n], var=to
        )
        copy.start()
        pat_copies.append(copy)
    own_rows = pl.ds(pl.multiple_of(me_t * rows, rows), rows)
    w_ref[own_rows, :width] = vw_ref[...]
    w_ref[own_rows, width:] = ow_ref[...]
    spot = (own_rows, pl.ds(pl.multiple_of(me_v * wide, wide), wide))
    tok_copies = []
    for n in range(1, n_tok):
        to = lax.rem(me_t + n, n_tok)
        copy = remote(w_ref.at[spot], w_ref.at[spot], tok_send.at[n], tok_recv.at[n], tok=to)
        copy.start()
        tok_copies.append(copy)

    head_of = lax.broadcasted_iota(jnp.int32, (H, width), 1) // HD
    heads = (head_of == lax.broadcasted_iota(jnp.int32, (H, width), 0)).astype(F32).astype(BF)
    seen = kw_ref[...].astype(F32) * query_ref[...].astype(F32)
    seen_hi = seen.astype(BF)
    seen_lo = (seen - seen_hi.astype(F32)).astype(BF)
    wqs_ref[...] = lax.dot_general(
        heads, seen_hi, NT, preferred_element_type=F32
    ) + lax.dot_general(heads, seen_lo, NT, preferred_element_type=F32)
    wq_copies = []
    for n in range(1, n_tok):
        to = lax.rem(me_t + n, n_tok)
        copy = remote(wqs_ref, wqa_ref.at[me_t], wq_send.at[n], wq_recv.at[n], tok=to)
        copy.start()
        wq_copies.append(copy)

    pixels_ref[me_v] = pat_ref[me_v]
    wqa_ref[me_t] = wqs_ref[...]
    acc_ref[...] = jnp.zeros_like(acc_ref)

    picker = (
        lax.broadcasted_iota(jnp.int32, (vars_, slots), 0) == slot_ref[...]
    ).astype(F32).astype(BF)

    def slot_rows(count, tall_one, copies):
        at = lax.broadcasted_iota(jnp.int32, (count, slots), 0)
        slot = lax.broadcasted_iota(jnp.int32, (count, slots), 1)
        within = at % tall_one
        live_row = within < copies * local_slots
        match = slot == (at // tall_one) * local_slots + within % local_slots
        return (live_row & match).astype(F32).astype(BF), within // local_slots

    row_copies = []
    sib_copies = []

    def to_sibling(n, m, spot):
        at = (n - 1) * pairs + m
        copy = remote(w_ref.at[spot], w_ref.at[spot], sib_send.at[at], sib_recv.at[at], var=sibling)
        copy.start()
        sib_copies.append(copy)

    def place_of(n, m):
        source = lax.rem(me_t + n_tok - n, n_tok)
        owner = lax.rem(me_v + n_var - 2 * m, n_var)
        return (
            pl.ds(pl.multiple_of(source * rows, rows), rows),
            pl.ds(pl.multiple_of(owner * wide, wide), wide),
        )

    def pass_first(n):
        tok_copies[n - 1].wait_recv()
        spot = place_of(n, 0)
        for m in range(1, pairs):
            at = (n - 1) * (pairs - 1) + m - 1
            to = lax.rem(me_v + 2 * m, n_var)
            copy = remote(w_ref.at[spot], w_ref.at[spot], row_send.at[at], row_recv.at[at], var=to)
            copy.start()
            row_copies.append(copy)
        to_sibling(n, 0, spot)

    def pass_second(n):
        for m in range(1, pairs):
            row_copies[(n - 1) * (pairs - 1) + m - 1].wait_recv()
            to_sibling(n, m, place_of(n, m))

    for copy in pat_copies:
        copy.wait_recv()
    held = pat_ref.shape[1]
    unpad, _ = slot_rows(n_var * held, held, 1)
    chooser = lax.dot_general(picker, unpad, NT, preferred_element_type=F32).astype(BF)
    live = jnp.dot(chooser, pixels_ref[...].reshape(n_var * held, -1), preferred_element_type=F32)
    lane_at = lax.broadcasted_iota(jnp.int32, live.shape, 1)

    def embed(first, count):
        @pl.loop(first, first + count)
        def _(t):
            cols = []
            for p in range(4):
                col = jnp.sum(
                    jnp.where(lane_at == p * toks + t, live, 0.0), axis=1, keepdims=True
                )
                pix_ref[t, :, p : p + 1] = col
                cols.append(col)
            for c in range(0, width, block):
                span = slice(c, c + block)
                pre = ve_ref[:, span].astype(F32)
                for p in range(4):
                    pre = pre + cols[p] * pw_ref[p, :, span]
                cdf = 0.5 * (1.0 + lax.erf(pre * inv_sqrt_two))
                e_ref[t, :, span] = (pre * cdf).astype(BF)
                slope_ref[t, :, span] = cdf + pre * jnp.exp(-0.5 * pre * pre) * inv_sqrt_two_pi

    def attend(first, count):
        flat = e_ref[first : first + count].reshape(count * vars_, width)
        both = lax.dot_general(flat, wq_both, NT, preferred_element_type=F32)
        both = both.reshape(count, vars_, 2 * H)
        raw = (both[:, :, :H] + both[:, :, H:]) * (1.0 / math.sqrt(HD))
        squashed = jnp.tanh(raw * (1.0 / score_cap))
        exp_scores = jnp.exp(score_cap * squashed)
        attn = exp_scores / jnp.sum(exp_scores, axis=1, keepdims=True)
        attn_ref[first : first + count] = attn
        slope_s_ref[first : first + count] = (
            attn * (1.0 - squashed * squashed) * (1.0 / math.sqrt(HD))
        )
        for u in range(count):
            mixed = lax.dot_general(
                attn[u].astype(BF), e_ref[first + u], TN, preferred_element_type=F32
            )
            for c in range(spans):
                cell = mixed[:, c * lanes : (c + 1) * lanes]
                pe_ref[pl.ds(c * tall + first + u, H, stride=toks), :] = cell

    steps = 8
    first_done, second_done = 1, 1
    for c in range(steps):
        each = toks // steps
        embed(c * each, each)
        if c == 0:
            for copy in wq_copies:
                copy.wait_recv()
            wq = jnp.concatenate([wqa_ref[k] for k in range(n_tok)], axis=1)
            wq_hi = wq.astype(BF)
            wq_lo = (wq - wq_hi.astype(F32)).astype(BF)
            wq_both = jnp.concatenate([wq_hi, wq_lo], axis=0)
        attend(c * each, each)
        upto = 1 + (c + 1) * (n_tok - 1) // steps
        while second_done < first_done:
            pass_second(second_done)
            second_done += 1
        while first_done < upto:
            pass_first(first_done)
            first_done += 1
    while second_done < first_done:
        pass_second(second_done)
        second_done += 1

    for copy in sib_copies:
        copy.wait_recv()

    gp = lax.dot_general(cot_ref[...], w_ref[:, width:], NT, preferred_element_type=F32)
    low = lax.broadcasted_iota(jnp.int32, (toks, 2 * HD), 1) < HD
    for pair in range(H // 2):
        part = gp[:, pair * 2 * HD : (pair + 1) * 2 * HD]
        both = jnp.concatenate([jnp.where(low, part, 0.0), jnp.where(low, 0.0, part)], axis=0)
        carried = lax.dot_general(
            both.astype(BF),
            w_ref[:, pair * 2 * HD : (pair + 1) * 2 * HD],
            NT,
            preferred_element_type=F32,
        )
        for c in range(spans):
            g_ref[pl.ds(c * tall + pair * 2 * toks, 2 * toks), :] = carried[
                :, c * lanes : (c + 1) * lanes
            ]

    def token_rows(t, first, count):
        cells = [g_ref[pl.ds(c * tall + t, H, stride=toks), :] for c in range(first, first + count)]
        return jnp.concatenate(cells, axis=1).astype(BF)

    group = 4

    @pl.loop(0, toks // group)
    def _(step):
        for u in range(group):
            t = step * group + u
            rhs = token_rows(t, 0, spans)
            s_ref[t] = lax.dot_general(e_ref[t], rhs, NT, preferred_element_type=F32)

    attn = attn_ref[...]
    grad_attn = s_ref[...]
    grad_raw = slope_s_ref[...] * (grad_attn - jnp.sum(attn * grad_attn, axis=1, keepdims=True))
    lhs_ref[...] = jnp.concatenate([attn, grad_raw], axis=2).astype(BF)

    cut = 4 * width // n_tok
    chunks = cut // lanes
    tall_out = in_ref.shape[1]
    place, chunk_of = slot_rows(n_var * tall_out, tall_out, chunks)
    placed = lax.dot_general(place, picker, NT, preferred_element_type=F32).astype(BF)
    chunk_of = chunk_of[:, :1]
    spread = jnp.concatenate(
        [jnp.where(chunk_of == c, placed, jnp.zeros_like(placed)) for c in range(chunks)], axis=1
    )
    half = width // 2
    per = half // cut
    count = 4 * per

    for h in range(2):

        @pl.loop(0, toks // group)
        def _(step):
            cols, left, right = [], [], []
            for u in range(group):
                t = step * group + u
                left.append(lhs_ref[t])
                mine = token_rows(t, h * spans // 2, spans // 2)
                right.append(
                    jnp.concatenate([mine, wq_hi[:, h * half : (h + 1) * half]], axis=0)
                )
                pix = pix_ref[t]
                cols.append([pix[:, p : p + 1] for p in range(4)])
            for c in range(0, half, block):
                span = slice(h * half + c, h * half + c + block)
                grads = [
                    jnp.dot(left[u], right[u][:, c : c + block], preferred_element_type=F32)
                    * slope_ref[step * group + u, :, span]
                    for u in range(group)
                ]
                for p in range(4):
                    more = cols[0][p] * grads[0]
                    for u in range(1, group):
                        more = more + cols[u][p] * grads[u]
                    acc_ref[p, :, span] += more

        for a in range(count):
            p, start = a // per, h * half + a % per * cut
            k = p * 2 * per + h * per + a % per
            stacked = jnp.concatenate(
                [
                    acc_ref[p, :, start + c * lanes : start + (c + 1) * lanes].astype(BF)
                    for c in range(chunks)
                ],
                axis=0,
            )
            out = jnp.dot(spread, stacked, preferred_element_type=F32).astype(BF)
            for i in range(n_var):
                out_ref[k * n_var + i] = out[i * tall_out : (i + 1) * tall_out]

        @pl.loop(0, count * n_var)
        def _(n):
            a = lax.rem(me_t // 2 + n // n_var, count)
            k = a // per * 2 * per + h * per + lax.rem(a, per)
            i = lax.rem(me_v + lax.rem(n, n_var), n_var)
            at = k * n_var + i

            @pl.when(at != me)
            def _():
                remote(
                    out_ref.at[at], in_ref.at[me], sum_send.at[at], sum_recv.at[me], tok=k, var=i
                ).start()

    pieces = []
    for pair in range(H // 2):
        both = jnp.concatenate(
            [pe_ref[pl.ds(c * tall + pair * 2 * toks, 2 * toks), :] for c in range(spans)],
            axis=1,
        ).astype(BF)
        two = jnp.dot(
            both, w_ref[:, pair * 2 * HD : (pair + 1) * 2 * HD], preferred_element_type=F32
        )
        pieces.append(jnp.where(low, two[:toks], two[toks:]))
    pooled = jnp.concatenate(pieces, axis=1).astype(BF)
    agg_ref[...] = jnp.dot(pooled, w_ref[:, width:], preferred_element_type=F32).astype(BF)

    total_ref[...] = out_ref[me].astype(F32)

    @pl.loop(1, total)
    def _(n):
        to = peer(n)
        at = to["tok"] * n_var + to["var"]
        copy = remote(out_ref.at[at], in_ref.at[at], sum_send.at[at], sum_recv.at[at], **to)
        copy.wait()
        total_ref[...] += in_ref[at].astype(F32)

    for c in range(chunks):
        sum_ref[:, c * lanes : (c + 1) * lanes] = total_ref[
            c * local_slots : (c + 1) * local_slots, :
        ]

    for copy in pat_copies + wq_copies + tok_copies + row_copies + sib_copies:
        copy.wait_send()


def compute(n_tok, n_var, pat, slot, query, kw, vw, ow, pw, ve, cot):
    toks, width = cot.shape
    vars_ = ve.shape[0]
    rows = vw.shape[0]
    local_slots = slot.shape[1] // n_var
    pairs = n_var // 2
    total = n_tok * n_var
    chunks = 4 * width // n_tok // 128
    tall_out = -(-chunks * local_slots // 16) * 16
    vm = pl.BlockSpec(memory_space=pltpu.VMEM)
    dma = pltpu.SemaphoreType.DMA
    return pl.pallas_call(
        functools.partial(all_kernel, n_tok, n_var),
        out_shape=(
            jax.ShapeDtypeStruct((toks, width), BF),
            jax.ShapeDtypeStruct((local_slots, chunks * 128), F32),
        ),
        in_specs=[vm] * 9,
        out_specs=(vm, vm),
        scratch_shapes=[
            pltpu.VMEM((tall_out, 128), F32),
            pltpu.VMEM(pat.shape, BF),
            pltpu.VMEM((H, rows), F32),
            pltpu.VMEM((n_tok, H, rows), F32),
            pltpu.VMEM((width, 2 * width), BF),
            pltpu.VMEM((toks, vars_, 4), F32),
            pltpu.VMEM((toks, vars_, width), BF),
            pltpu.VMEM((toks, vars_, width), F32),
            pltpu.VMEM((width // 128 * H * toks, 128), F32),
            pltpu.VMEM((toks, vars_, H), F32),
            pltpu.VMEM((toks, vars_, H), F32),
            pltpu.VMEM((toks, vars_, H), F32),
            pltpu.VMEM((toks, vars_, 2 * H), BF),
            pltpu.VMEM((width // 128 * H * toks, 128), F32),
            pltpu.VMEM((4, vars_, width), F32),
            pltpu.VMEM((total, tall_out, 128), BF),
            pltpu.VMEM((total, tall_out, 128), BF),
            dma((n_var,)),
            dma((n_var,)),
            dma((n_tok,)),
            dma((n_tok,)),
            dma((n_tok,)),
            dma((n_tok,)),
            dma((n_tok * pairs,)),
            dma((n_tok * pairs,)),
            dma((n_tok * pairs,)),
            dma((n_tok * pairs,)),
            dma((total,)),
            dma((total,)),
        ],
        compiler_params=pltpu.CompilerParams(
            vmem_limit_bytes=56 * 1024 * 1024, collective_id=0, has_side_effects=True
        ),
    )(pat, slot, query, kw, vw, ow, pw, ve, cot)


def body(
    n_tok,
    n_var,
    patches,
    slot_var,
    patch_weight,
    var_embed,
    query,
    key_weight,
    value_weight,
    out_weight,
    cotangent,
):
    local_slots = patches.shape[0]
    toks = cotangent.shape[0]
    mine = patches.reshape(local_slots, 4, n_var, toks).transpose(2, 0, 1, 3)
    mine = mine.reshape(n_var, local_slots, 4 * toks)
    mine = jnp.pad(mine, ((0, 0), (0, -local_slots % 16), (0, 0)))
    return compute(
        n_tok,
        n_var,
        mine,
        slot_var.reshape(1, -1),
        query.reshape(1, -1),
        key_weight,
        value_weight,
        out_weight,
        patch_weight.transpose(1, 0, 2).astype(F32),
        var_embed,
        cotangent,
    )


def solution(mesh):
    return jax.shard_map(
        functools.partial(body, mesh.shape["tok"], mesh.shape["var"]),
        mesh=mesh,
        in_specs=(
            P("var", None, "tok"),
            P(),
            P(),
            P(),
            P(),
            P("tok", None),
            P("tok", None),
            P("tok", None),
            P(("tok", "var"), None),
        ),
        out_specs=(P(("tok", "var"), None), P("var", "tok")),
        check_vma=False,
    )
```

```python
import functools
import math

import jax
import jax.numpy as jnp
from jax import lax
from jax.experimental import pallas as pl
from jax.experimental.pallas import tpu as pltpu
from jax.sharding import PartitionSpec as P

H = 16
HD = 64

score_cap = 5.0
inv_sqrt_two = 1.0 / math.sqrt(2.0)
inv_sqrt_two_pi = 1.0 / math.sqrt(2.0 * math.pi)

BF = jnp.bfloat16
F32 = jnp.float32
NT = (((1,), (1,)), ((), ()))
TN = (((0,), (0,)), ((), ()))


def all_kernel(
    n_tok,
    n_var,
    pat_ref,
    slot_ref,
    query_ref,
    kw_ref,
    vw_ref,
    ow_ref,
    pw_ref,
    ve_ref,
    cot_ref,
    agg_ref,
    sum_ref,
    total_ref,
    pixels_ref,
    wqs_ref,
    wqa_ref,
    w_ref,
    pix_ref,
    e_ref,
    slope_ref,
    g_ref,
    attn_ref,
    slope_s_ref,
    wqb_ref,
    pooled_ref,
    lhs_ref,
    pe_ref,
    acc_ref,
    out_ref,
    in_ref,
    pat_send,
    pat_recv,
    wq_send,
    wq_recv,
    tok_send,
    tok_recv,
    row_send,
    row_recv,
    sib_send,
    sib_recv,
    sum_send,
    sum_recv,
):
    toks, width = cot_ref.shape
    rows = vw_ref.shape[0]
    vars_ = ve_ref.shape[0]
    slots = slot_ref.shape[1]
    local_slots = slots // n_var
    lanes = 128
    spans = width // lanes
    tall = H * toks
    total = n_tok * n_var
    wide = 2 * width // n_var
    pairs = n_var // 2
    block = 256
    me_t = lax.axis_index("tok")
    me_v = lax.axis_index("var")
    me = me_t * n_var + me_v
    sibling = me_v + 1 - 2 * lax.rem(me_v, 2)

    def remote(src, dst, send, recv, **place):
        return pltpu.make_async_remote_copy(
            src_ref=src,
            dst_ref=dst,
            send_sem=send,
            recv_sem=recv,
            device_id=place,
            device_id_type=pl.DeviceIdType.MESH,
        )

    def peer(n):
        at = lax.rem(me + n, total)
        return {"tok": at // n_var, "var": lax.rem(at, n_var)}

    barrier = pltpu.get_barrier_semaphore()

    @pl.loop(1, total)
    def _(n):
        pl.semaphore_signal(
            barrier, inc=1, device_id=peer(n), device_id_type=pl.DeviceIdType.MESH
        )

    pl.semaphore_wait(barrier, total - 1)

    pat_copies = []
    for n in range(1, n_var):
        to = lax.rem(me_v + n, n_var)
        copy = remote(
            pat_ref.at[to], pixels_ref.at[me_v], pat_send.at[n], pat_recv.at[n], var=to
        )
        copy.start()
        pat_copies.append(copy)
    own_rows = pl.ds(pl.multiple_of(me_t * rows, rows), rows)
    w_ref[own_rows, :width] = vw_ref[...]
    w_ref[own_rows, width:] = ow_ref[...]
    spot = (own_rows, pl.ds(pl.multiple_of(me_v * wide, wide), wide))

    def offset(j):
        odd = lax.rem(j, 2)
        return odd * ((j + 1) // 2) + (1 - odd) * (n_tok - j // 2)

    def tok_copy(n):
        to = lax.rem(me_t + n, n_tok)
        return remote(w_ref.at[spot], w_ref.at[spot], tok_send.at[n], tok_recv.at[n], tok=to)

    def wq_copy(n):
        to = lax.rem(me_t + n, n_tok)
        return remote(wqs_ref, wqa_ref.at[me_t], wq_send.at[n], wq_recv.at[n], tok=to)

    @pl.loop(1, n_tok)
    def _(j):
        tok_copy(offset(j)).start()

    head_of = lax.broadcasted_iota(jnp.int32, (H, width), 1) // HD
    heads = (head_of == lax.broadcasted_iota(jnp.int32, (H, width), 0)).astype(F32).astype(BF)
    seen = kw_ref[...].astype(F32) * query_ref[...].astype(F32)
    seen_hi = seen.astype(BF)
    seen_lo = (seen - seen_hi.astype(F32)).astype(BF)
    wqs_ref[...] = lax.dot_general(
        heads, seen_hi, NT, preferred_element_type=F32
    ) + lax.dot_general(heads, seen_lo, NT, preferred_element_type=F32)

    @pl.loop(1, n_tok)
    def _(j):
        wq_copy(offset(j)).start()

    pixels_ref[me_v] = pat_ref[me_v]
    wqa_ref[me_t] = wqs_ref[...]
    acc_ref[...] = jnp.zeros_like(acc_ref)

    picker = (
        lax.broadcasted_iota(jnp.int32, (vars_, slots), 0) == slot_ref[...]
    ).astype(F32).astype(BF)

    def slot_rows(count, tall_one, copies):
        at = lax.broadcasted_iota(jnp.int32, (count, slots), 0)
        slot = lax.broadcasted_iota(jnp.int32, (count, slots), 1)
        within = at % tall_one
        live_row = within < copies * local_slots
        match = slot == (at // tall_one) * local_slots + within % local_slots
        return (live_row & match).astype(F32).astype(BF), within // local_slots

    def place_of(n, m):
        source = lax.rem(me_t + n_tok - n, n_tok)
        owner = lax.rem(me_v + n_var - 2 * m, n_var)
        return (
            pl.ds(pl.multiple_of(source * rows, rows), rows),
            pl.ds(pl.multiple_of(owner * wide, wide), wide),
        )

    def sib_copy(n, m):
        where = place_of(n, m)
        at = (n - 1) * pairs + m
        return remote(w_ref.at[where], w_ref.at[where], sib_send.at[at], sib_recv.at[at], var=sibling)

    def row_copy(n, m):
        where = place_of(n, 0)
        at = (n - 1) * (pairs - 1) + m - 1
        to = lax.rem(me_v + 2 * m, n_var)
        return remote(w_ref.at[where], w_ref.at[where], row_send.at[at], row_recv.at[at], var=to)

    def pass_first(first, last):
        @pl.loop(first, last)
        def _(j):
            n = offset(j)
            tok_copy(n).wait_recv()
            for m in range(1, pairs):
                row_copy(n, m).start()
            sib_copy(n, 0).start()

    def pass_second(first, last):
        @pl.loop(first, last)
        def _(j):
            n = offset(j)
            for m in range(1, pairs):
                row_copy(n, m).wait_recv()
                sib_copy(n, m).start()

    for copy in pat_copies:
        copy.wait_recv()
    held = pat_ref.shape[1]
    unpad, _ = slot_rows(n_var * held, held, 1)
    chooser = lax.dot_general(picker, unpad, NT, preferred_element_type=F32).astype(BF)
    live = jnp.dot(chooser, pixels_ref[...].reshape(n_var * held, -1), preferred_element_type=F32)
    lane_at = lax.broadcasted_iota(jnp.int32, live.shape, 1)

    def passed(t):
        return lax.max(t + 1, 0) * (n_tok - 1) // toks

    lag = 4

    @pl.loop(0, toks)
    def _(t):
        cols = []
        for p in range(4):
            col = jnp.sum(jnp.where(lane_at == p * toks + t, live, 0.0), axis=1, keepdims=True)
            pix_ref[t, :, p : p + 1] = col
            cols.append(col)

        @pl.loop(0, width // block)
        def _(c):
            span = pl.ds(pl.multiple_of(c * block, block), block)
            pre = ve_ref[:, span].astype(F32)
            for p in range(4):
                pre = pre + cols[p] * pw_ref[p, :, span]
            cdf = 0.5 * (1.0 + lax.erf(pre * inv_sqrt_two))
            e_ref[t, :, span] = (pre * cdf).astype(BF)
            slope_ref[t, :, span] = cdf + pre * jnp.exp(-0.5 * pre * pre) * inv_sqrt_two_pi

        pass_second(passed(t - lag - 1) + 1, passed(t - lag) + 1)
        pass_first(passed(t - 1) + 1, passed(t) + 1)

    @pl.loop(1, n_tok)
    def _(n):
        wq_copy(n).wait_recv()

    wq = jnp.concatenate([wqa_ref[k] for k in range(n_tok)], axis=1)
    wq_hi = wq.astype(BF)
    wqb_ref[:H] = wq_hi
    wqb_ref[H:] = (wq - wq_hi.astype(F32)).astype(BF)
    pass_second((toks - lag) * (n_tok - 1) // toks + 1, n_tok)

    group = 4

    @pl.loop(0, toks // group)
    def _(step):
        first = step * group
        flat = e_ref[pl.ds(first, group)].reshape(group * vars_, width)
        both = lax.dot_general(flat, wqb_ref[...], NT, preferred_element_type=F32)
        both = both.reshape(group, vars_, 2 * H)
        raw = (both[:, :, :H] + both[:, :, H:]) * (1.0 / math.sqrt(HD))
        squashed = jnp.tanh(raw * (1.0 / score_cap))
        exp_scores = jnp.exp(score_cap * squashed)
        attn = exp_scores / jnp.sum(exp_scores, axis=1, keepdims=True)
        attn_ref[pl.ds(first, group)] = attn
        slope_s_ref[pl.ds(first, group)] = (
            attn * (1.0 - squashed * squashed) * (1.0 / math.sqrt(HD))
        )
        for u in range(group):
            mixed = lax.dot_general(
                attn[u].astype(BF), e_ref[first + u], TN, preferred_element_type=F32
            )
            for c in range(spans):
                cell = mixed[:, c * lanes : (c + 1) * lanes]
                pe_ref[pl.ds(c * tall + first + u, H, stride=toks), :] = cell

    @pl.loop(1, n_tok)
    def _(n):
        for m in range(pairs):
            sib_copy(n, m).wait_recv()

    low = lax.broadcasted_iota(jnp.int32, (toks, 2 * HD), 1) < HD

    @pl.loop(0, H // 2)
    def _(pair):
        cols = pl.ds(pl.multiple_of(pair * 2 * HD, 2 * HD), 2 * HD)
        part = lax.dot_general(cot_ref[...], w_ref[cols, width:], NT, preferred_element_type=F32)
        both = jnp.concatenate([jnp.where(low, part, 0.0), jnp.where(low, 0.0, part)], axis=0)
        carried = lax.dot_general(both.astype(BF), w_ref[:, cols], NT, preferred_element_type=F32)
        for c in range(spans):
            at = pl.multiple_of(c * tall + pair * 2 * toks, 2 * toks)
            g_ref[pl.ds(at, 2 * toks), :] = carried[:, c * lanes : (c + 1) * lanes]

    def token_rows(t, first, count):
        cells = [g_ref[pl.ds(c * tall + t, H, stride=toks), :] for c in range(first, first + count)]
        return jnp.concatenate(cells, axis=1).astype(BF)

    @pl.loop(0, toks // group)
    def _(step):
        for u in range(group):
            t = step * group + u
            grad_attn = lax.dot_general(
                e_ref[t], token_rows(t, 0, spans), NT, preferred_element_type=F32
            )
            attn = attn_ref[t]
            mean = jnp.sum(attn * grad_attn, axis=0, keepdims=True)
            lhs_ref[t] = jnp.concatenate(
                [attn, slope_s_ref[t] * (grad_attn - mean)], axis=1
            ).astype(BF)

    cut = 4 * width // n_tok
    chunks = cut // lanes
    tall_out = in_ref.shape[1]
    place, chunk_of = slot_rows(n_var * tall_out, tall_out, chunks)
    placed = lax.dot_general(place, picker, NT, preferred_element_type=F32).astype(BF)
    chunk_of = chunk_of[:, :1]
    spread = jnp.concatenate(
        [jnp.where(chunk_of == c, placed, jnp.zeros_like(placed)) for c in range(chunks)], axis=1
    )
    half = width // 2
    per = half // cut
    count = 4 * per

    for h in range(2):

        @pl.loop(0, toks // group)
        def _(step):
            cols, left, right = [], [], []
            for u in range(group):
                t = step * group + u
                left.append(lhs_ref[t])
                mine = token_rows(t, h * spans // 2, spans // 2)
                right.append(
                    jnp.concatenate([mine, wqb_ref[:H, h * half : (h + 1) * half]], axis=0)
                )
                pix = pix_ref[t]
                cols.append([pix[:, p : p + 1] for p in range(4)])
            for c in range(0, half, block):
                span = slice(h * half + c, h * half + c + block)
                grads = [
                    jnp.dot(left[u], right[u][:, c : c + block], preferred_element_type=F32)
                    * slope_ref[step * group + u, :, span]
                    for u in range(group)
                ]
                for p in range(4):
                    more = cols[0][p] * grads[0]
                    for u in range(1, group):
                        more = more + cols[u][p] * grads[u]
                    acc_ref[p, :, span] += more

        for a in range(count):
            p, start = a // per, h * half + a % per * cut
            k = p * 2 * per + h * per + a % per
            stacked = jnp.concatenate(
                [
                    acc_ref[p, :, start + c * lanes : start + (c + 1) * lanes].astype(BF)
                    for c in range(chunks)
                ],
                axis=0,
            )
            out = jnp.dot(spread, stacked, preferred_element_type=F32).astype(BF)
            for i in range(n_var):
                out_ref[k * n_var + i] = out[i * tall_out : (i + 1) * tall_out]

        @pl.loop(0, count * n_var)
        def _(n):
            a = lax.rem(me_t // 2 + n // n_var, count)
            k = a // per * 2 * per + h * per + lax.rem(a, per)
            i = lax.rem(me_v + lax.rem(n, n_var), n_var)
            at = k * n_var + i

            @pl.when(at != me)
            def _():
                remote(
                    out_ref.at[at], in_ref.at[me], sum_send.at[at], sum_recv.at[me], tok=k, var=i
                ).start()

    @pl.loop(0, H // 2)
    def _(pair):
        cols = pl.ds(pl.multiple_of(pair * 2 * HD, 2 * HD), 2 * HD)
        both = jnp.concatenate(
            [
                pe_ref[pl.ds(pl.multiple_of(c * tall + pair * 2 * toks, 2 * toks), 2 * toks), :]
                for c in range(spans)
            ],
            axis=1,
        ).astype(BF)
        two = jnp.dot(both, w_ref[:, cols], preferred_element_type=F32)
        pooled_ref[:, cols] = jnp.where(low, two[:toks], two[toks:]).astype(BF)

    @pl.loop(0, width // block)
    def _(c):
        at = pl.multiple_of(c * block, block)
        agg_ref[:, pl.ds(at, block)] = jnp.dot(
            pooled_ref[...], w_ref[:, pl.ds(width + at, block)], preferred_element_type=F32
        ).astype(BF)

    total_ref[...] = out_ref[me].astype(F32)

    @pl.loop(1, total)
    def _(n):
        to = peer(n)
        at = to["tok"] * n_var + to["var"]
        copy = remote(out_ref.at[at], in_ref.at[at], sum_send.at[at], sum_recv.at[at], **to)
        copy.wait()
        total_ref[...] += in_ref[at].astype(F32)

    for c in range(chunks):
        sum_ref[:, c * lanes : (c + 1) * lanes] = total_ref[
            c * local_slots : (c + 1) * local_slots, :
        ]

    for copy in pat_copies:
        copy.wait_send()

    @pl.loop(1, n_tok)
    def _(n):
        wq_copy(n).wait_send()
        tok_copy(n).wait_send()
        for m in range(1, pairs):
            row_copy(n, m).wait_send()
        for m in range(pairs):
            sib_copy(n, m).wait_send()


def compute(n_tok, n_var, pat, slot, query, kw, vw, ow, pw, ve, cot):
    toks, width = cot.shape
    vars_ = ve.shape[0]
    rows = vw.shape[0]
    local_slots = slot.shape[1] // n_var
    pairs = n_var // 2
    total = n_tok * n_var
    chunks = 4 * width // n_tok // 128
    tall_out = -(-chunks * local_slots // 16) * 16
    vm = pl.BlockSpec(memory_space=pltpu.VMEM)
    dma = pltpu.SemaphoreType.DMA
    return pl.pallas_call(
        functools.partial(all_kernel, n_tok, n_var),
        out_shape=(
            jax.ShapeDtypeStruct((toks, width), BF),
            jax.ShapeDtypeStruct((local_slots, chunks * 128), F32),
        ),
        in_specs=[vm] * 9,
        out_specs=(vm, vm),
        scratch_shapes=[
            pltpu.VMEM((tall_out, 128), F32),
            pltpu.VMEM(pat.shape, BF),
            pltpu.VMEM((H, rows), F32),
            pltpu.VMEM((n_tok, H, rows), F32),
            pltpu.VMEM((width, 2 * width), BF),
            pltpu.VMEM((toks, vars_, 4), F32),
            pltpu.VMEM((toks, vars_, width), BF),
            pltpu.VMEM((toks, vars_, width), F32),
            pltpu.VMEM((width // 128 * H * toks, 128), F32),
            pltpu.VMEM((toks, vars_, H), F32),
            pltpu.VMEM((toks, vars_, H), F32),
            pltpu.VMEM((2 * H, width), BF),
            pltpu.VMEM((toks, width), BF),
            pltpu.VMEM((toks, vars_, 2 * H), BF),
            pltpu.VMEM((width // 128 * H * toks, 128), F32),
            pltpu.VMEM((4, vars_, width), F32),
            pltpu.VMEM((total, tall_out, 128), BF),
            pltpu.VMEM((total, tall_out, 128), BF),
            dma((n_var,)),
            dma((n_var,)),
            dma((n_tok,)),
            dma((n_tok,)),
            dma((n_tok,)),
            dma((n_tok,)),
            dma((n_tok * pairs,)),
            dma((n_tok * pairs,)),
            dma((n_tok * pairs,)),
            dma((n_tok * pairs,)),
            dma((total,)),
            dma((total,)),
        ],
        compiler_params=pltpu.CompilerParams(
            vmem_limit_bytes=56 * 1024 * 1024, collective_id=0, has_side_effects=True
        ),
    )(pat, slot, query, kw, vw, ow, pw, ve, cot)


def body(
    n_tok,
    n_var,
    patches,
    slot_var,
    patch_weight,
    var_embed,
    query,
    key_weight,
    value_weight,
    out_weight,
    cotangent,
):
    local_slots = patches.shape[0]
    toks = cotangent.shape[0]
    mine = patches.reshape(local_slots, 4, n_var, toks).transpose(2, 0, 1, 3)
    mine = mine.reshape(n_var, local_slots, 4 * toks)
    mine = jnp.pad(mine, ((0, 0), (0, -local_slots % 16), (0, 0)))
    return compute(
        n_tok,
        n_var,
        mine,
        slot_var.reshape(1, -1),
        query.reshape(1, -1),
        key_weight,
        value_weight,
        out_weight,
        patch_weight.transpose(1, 0, 2).astype(F32),
        var_embed,
        cotangent,
    )


def solution(mesh):
    return jax.shard_map(
        functools.partial(body, mesh.shape["tok"], mesh.shape["var"]),
        mesh=mesh,
        in_specs=(
            P("var", None, "tok"),
            P(),
            P(),
            P(),
            P(),
            P("tok", None),
            P("tok", None),
            P("tok", None),
            P(("tok", "var"), None),
        ),
        out_specs=(P(("tok", "var"), None), P("var", "tok")),
        check_vma=False,
    )
```

```python
import functools
import math

import jax
import jax.numpy as jnp
from jax import lax
from jax.experimental import pallas as pl
from jax.experimental.pallas import tpu as pltpu
from jax.sharding import PartitionSpec as P

H = 16
HD = 64

score_cap = 5.0
inv_sqrt_two = 1.0 / math.sqrt(2.0)
inv_sqrt_two_pi = 1.0 / math.sqrt(2.0 * math.pi)

BF = jnp.bfloat16
F32 = jnp.float32
NT = (((1,), (1,)), ((), ()))
TN = (((0,), (0,)), ((), ()))


def all_kernel(
    n_tok,
    n_var,
    pat_ref,
    slot_ref,
    query_ref,
    kw_ref,
    vw_ref,
    ow_ref,
    pw_ref,
    ve_ref,
    cot_ref,
    agg_ref,
    sum_ref,
    total_ref,
    pixels_ref,
    wqs_ref,
    wqa_ref,
    w_ref,
    pix_ref,
    e_ref,
    slope_ref,
    g_ref,
    attn_ref,
    slope_s_ref,
    wqb_ref,
    pooled_ref,
    lhs_ref,
    pe_ref,
    acc_ref,
    out_ref,
    in_ref,
    pat_send,
    pat_recv,
    wq_send,
    wq_recv,
    tok_send,
    tok_recv,
    row_send,
    row_recv,
    sib_send,
    sib_recv,
    sum_send,
    sum_recv,
):
    toks, width = cot_ref.shape
    rows = vw_ref.shape[0]
    vars_ = ve_ref.shape[0]
    slots = slot_ref.shape[1]
    local_slots = slots // n_var
    lanes = 128
    spans = width // lanes
    tall = H * toks
    total = n_tok * n_var
    wide = 2 * width // n_var
    pairs = n_var // 2
    block = 256
    me_t = lax.axis_index("tok")
    me_v = lax.axis_index("var")
    me = me_t * n_var + me_v
    sibling = me_v + 1 - 2 * lax.rem(me_v, 2)

    def remote(src, dst, send, recv, **place):
        return pltpu.make_async_remote_copy(
            src_ref=src,
            dst_ref=dst,
            send_sem=send,
            recv_sem=recv,
            device_id=place,
            device_id_type=pl.DeviceIdType.MESH,
        )

    def peer(n):
        at = lax.rem(me + n, total)
        return {"tok": at // n_var, "var": lax.rem(at, n_var)}

    barrier = pltpu.get_barrier_semaphore()

    @pl.loop(1, total)
    def _(n):
        pl.semaphore_signal(
            barrier, inc=1, device_id=peer(n), device_id_type=pl.DeviceIdType.MESH
        )

    pl.semaphore_wait(barrier, total - 1)

    pat_copies = []
    for n in range(1, n_var):
        to = lax.rem(me_v + n, n_var)
        copy = remote(
            pat_ref.at[to], pixels_ref.at[me_v], pat_send.at[n], pat_recv.at[n], var=to
        )
        copy.start()
        pat_copies.append(copy)
    own_rows = pl.ds(pl.multiple_of(me_t * rows, rows), rows)
    w_ref[own_rows, :width] = vw_ref[...]
    w_ref[own_rows, width:] = ow_ref[...]
    spot = (own_rows, pl.ds(pl.multiple_of(me_v * wide, wide), wide))

    def offset(j):
        odd = lax.rem(j, 2)
        return odd * ((j + 1) // 2) + (1 - odd) * (n_tok - j // 2)

    def tok_copy(n):
        to = lax.rem(me_t + n, n_tok)
        return remote(w_ref.at[spot], w_ref.at[spot], tok_send.at[n], tok_recv.at[n], tok=to)

    def wq_copy(n):
        to = lax.rem(me_t + n, n_tok)
        return remote(wqs_ref, wqa_ref.at[me_t], wq_send.at[n], wq_recv.at[n], tok=to)

    @pl.loop(1, n_tok)
    def _(j):
        tok_copy(offset(j)).start()

    head_of = lax.broadcasted_iota(jnp.int32, (H, width), 1) // HD
    heads = (head_of == lax.broadcasted_iota(jnp.int32, (H, width), 0)).astype(F32).astype(BF)
    seen = kw_ref[...].astype(F32) * query_ref[...].astype(F32)
    seen_hi = seen.astype(BF)
    seen_lo = (seen - seen_hi.astype(F32)).astype(BF)
    wqs_ref[...] = lax.dot_general(
        heads, seen_hi, NT, preferred_element_type=F32
    ) + lax.dot_general(heads, seen_lo, NT, preferred_element_type=F32)

    @pl.loop(1, n_tok)
    def _(j):
        wq_copy(offset(j)).start()

    pixels_ref[me_v] = pat_ref[me_v]
    wqa_ref[me_t] = wqs_ref[...]
    acc_ref[...] = jnp.zeros_like(acc_ref)

    picker = (
        lax.broadcasted_iota(jnp.int32, (vars_, slots), 0) == slot_ref[...]
    ).astype(F32).astype(BF)

    def slot_rows(count, tall_one, copies):
        at = lax.broadcasted_iota(jnp.int32, (count, slots), 0)
        slot = lax.broadcasted_iota(jnp.int32, (count, slots), 1)
        within = at % tall_one
        live_row = within < copies * local_slots
        match = slot == (at // tall_one) * local_slots + within % local_slots
        return (live_row & match).astype(F32).astype(BF), within // local_slots

    def place_of(n, m):
        source = lax.rem(me_t + n_tok - n, n_tok)
        owner = lax.rem(me_v + n_var - 2 * m, n_var)
        return (
            pl.ds(pl.multiple_of(source * rows, rows), rows),
            pl.ds(pl.multiple_of(owner * wide, wide), wide),
        )

    def sib_copy(n, m):
        where = place_of(n, m)
        at = (n - 1) * pairs + m
        return remote(w_ref.at[where], w_ref.at[where], sib_send.at[at], sib_recv.at[at], var=sibling)

    def row_copy(n, m):
        where = place_of(n, 0)
        at = (n - 1) * (pairs - 1) + m - 1
        to = lax.rem(me_v + 2 * m, n_var)
        return remote(w_ref.at[where], w_ref.at[where], row_send.at[at], row_recv.at[at], var=to)

    def pass_first(first, last):
        @pl.loop(first, last)
        def _(j):
            n = offset(j)
            tok_copy(n).wait_recv()
            for m in range(1, pairs):
                row_copy(n, m).start()
            sib_copy(n, 0).start()

    def pass_second(first, last):
        @pl.loop(first, last)
        def _(j):
            n = offset(j)
            for m in range(1, pairs):
                row_copy(n, m).wait_recv()
                sib_copy(n, m).start()

    for copy in pat_copies:
        copy.wait_recv()
    held = pat_ref.shape[1]
    unpad, _ = slot_rows(n_var * held, held, 1)
    chooser = lax.dot_general(picker, unpad, NT, preferred_element_type=F32).astype(BF)
    live = jnp.dot(chooser, pixels_ref[...].reshape(n_var * held, -1), preferred_element_type=F32)
    lane_at = lax.broadcasted_iota(jnp.int32, live.shape, 1)

    def passed(t):
        return lax.max(t + 1, 0) * (n_tok - 1) // toks

    lag = 4

    @pl.loop(0, toks)
    def _(t):
        cols = []
        for p in range(4):
            col = jnp.sum(jnp.where(lane_at == p * toks + t, live, 0.0), axis=1, keepdims=True)
            pix_ref[t, :, p : p + 1] = col
            cols.append(col)

        @pl.loop(0, width // block)
        def _(c):
            span = pl.ds(pl.multiple_of(c * block, block), block)
            pre = ve_ref[:, span].astype(F32)
            for p in range(4):
                pre = pre + cols[p] * pw_ref[p, :, span]
            cdf = 0.5 * (1.0 + lax.erf(pre * inv_sqrt_two))
            e_ref[t, :, span] = (pre * cdf).astype(BF)
            slope_ref[t, :, span] = cdf + pre * jnp.exp(-0.5 * pre * pre) * inv_sqrt_two_pi

        pass_second(passed(t - lag - 1) + 1, passed(t - lag) + 1)
        pass_first(passed(t - 1) + 1, passed(t) + 1)

    @pl.loop(1, n_tok)
    def _(n):
        wq_copy(n).wait_recv()

    wq = jnp.concatenate([wqa_ref[k] for k in range(n_tok)], axis=1)
    wq_hi = wq.astype(BF)
    wqb_ref[:H] = wq_hi
    wqb_ref[H:] = (wq - wq_hi.astype(F32)).astype(BF)
    pass_second((toks - lag) * (n_tok - 1) // toks + 1, n_tok)

    group = 4
    many = 8

    @pl.loop(0, toks // many)
    def _(step):
        first = step * many
        flat = e_ref[pl.ds(first, many)].reshape(many * vars_, width)
        both = lax.dot_general(flat, wqb_ref[...], NT, preferred_element_type=F32)
        both = both.reshape(many, vars_, 2 * H)
        raw = (both[:, :, :H] + both[:, :, H:]) * (1.0 / math.sqrt(HD))
        squashed = jnp.tanh(raw * (1.0 / score_cap))
        exp_scores = jnp.exp(score_cap * squashed)
        attn = exp_scores / jnp.sum(exp_scores, axis=1, keepdims=True)
        attn_ref[pl.ds(first, many)] = attn
        slope_s_ref[pl.ds(first, many)] = (
            attn * (1.0 - squashed * squashed) * (1.0 / math.sqrt(HD))
        )
        for u in range(many):
            mixed = lax.dot_general(
                attn[u].astype(BF), e_ref[first + u], TN, preferred_element_type=F32
            )
            for c in range(spans):
                cell = mixed[:, c * lanes : (c + 1) * lanes]
                pe_ref[pl.ds(c * tall + first + u, H, stride=toks), :] = cell

    @pl.loop(1, n_tok)
    def _(n):
        for m in range(pairs):
            sib_copy(n, m).wait_recv()

    low = lax.broadcasted_iota(jnp.int32, (toks, 2 * HD), 1) < HD

    @pl.loop(0, H // 2)
    def _(pair):
        cols = pl.ds(pl.multiple_of(pair * 2 * HD, 2 * HD), 2 * HD)
        part = lax.dot_general(cot_ref[...], w_ref[cols, width:], NT, preferred_element_type=F32)
        both = jnp.concatenate([jnp.where(low, part, 0.0), jnp.where(low, 0.0, part)], axis=0)
        carried = lax.dot_general(both.astype(BF), w_ref[:, cols], NT, preferred_element_type=F32)
        for c in range(spans):
            at = pl.multiple_of(c * tall + pair * 2 * toks, 2 * toks)
            g_ref[pl.ds(at, 2 * toks), :] = carried[:, c * lanes : (c + 1) * lanes]

    def token_rows(t, first, count):
        cells = [g_ref[pl.ds(c * tall + t, H, stride=toks), :] for c in range(first, first + count)]
        return jnp.concatenate(cells, axis=1).astype(BF)

    @pl.loop(0, toks // many)
    def _(step):
        for u in range(many):
            t = step * many + u
            grad_attn = lax.dot_general(
                e_ref[t], token_rows(t, 0, spans), NT, preferred_element_type=F32
            )
            attn = attn_ref[t]
            mean = jnp.sum(attn * grad_attn, axis=0, keepdims=True)
            lhs_ref[t] = jnp.concatenate(
                [attn, slope_s_ref[t] * (grad_attn - mean)], axis=1
            ).astype(BF)

    cut = 4 * width // n_tok
    chunks = cut // lanes
    tall_out = in_ref.shape[1]
    place, chunk_of = slot_rows(n_var * tall_out, tall_out, chunks)
    placed = lax.dot_general(place, picker, NT, preferred_element_type=F32).astype(BF)
    chunk_of = chunk_of[:, :1]
    spread = jnp.concatenate(
        [jnp.where(chunk_of == c, placed, jnp.zeros_like(placed)) for c in range(chunks)], axis=1
    )
    half = width // 2
    per = half // cut
    count = 4 * per

    for h in range(2):

        @pl.loop(0, toks // group)
        def _(step):
            cols, left, right = [], [], []
            for u in range(group):
                t = step * group + u
                left.append(lhs_ref[t])
                mine = token_rows(t, h * spans // 2, spans // 2)
                right.append(
                    jnp.concatenate([mine, wqb_ref[:H, h * half : (h + 1) * half]], axis=0)
                )
                pix = pix_ref[t]
                cols.append([pix[:, p : p + 1] for p in range(4)])
            for c in range(0, half, block):
                span = slice(h * half + c, h * half + c + block)
                grads = [
                    jnp.dot(left[u], right[u][:, c : c + block], preferred_element_type=F32)
                    * slope_ref[step * group + u, :, span]
                    for u in range(group)
                ]
                for p in range(4):
                    more = cols[0][p] * grads[0]
                    for u in range(1, group):
                        more = more + cols[u][p] * grads[u]
                    acc_ref[p, :, span] += more

        for a in range(count):
            p, start = a // per, h * half + a % per * cut
            k = p * 2 * per + h * per + a % per
            stacked = jnp.concatenate(
                [
                    acc_ref[p, :, start + c * lanes : start + (c + 1) * lanes].astype(BF)
                    for c in range(chunks)
                ],
                axis=0,
            )
            out = jnp.dot(spread, stacked, preferred_element_type=F32).astype(BF)
            for i in range(n_var):
                out_ref[k * n_var + i] = out[i * tall_out : (i + 1) * tall_out]

        @pl.loop(0, count * n_var)
        def _(n):
            a = lax.rem(me_t // 2 + n // n_var, count)
            k = a // per * 2 * per + h * per + lax.rem(a, per)
            i = lax.rem(me_v + lax.rem(n, n_var), n_var)
            at = k * n_var + i

            @pl.when(at != me)
            def _():
                remote(
                    out_ref.at[at], in_ref.at[me], sum_send.at[at], sum_recv.at[me], tok=k, var=i
                ).start()

    @pl.loop(0, H // 2)
    def _(pair):
        cols = pl.ds(pl.multiple_of(pair * 2 * HD, 2 * HD), 2 * HD)
        both = jnp.concatenate(
            [
                pe_ref[pl.ds(pl.multiple_of(c * tall + pair * 2 * toks, 2 * toks), 2 * toks), :]
                for c in range(spans)
            ],
            axis=1,
        ).astype(BF)
        two = jnp.dot(both, w_ref[:, cols], preferred_element_type=F32)
        pooled_ref[:, cols] = jnp.where(low, two[:toks], two[toks:]).astype(BF)

    @pl.loop(0, width // block)
    def _(c):
        at = pl.multiple_of(c * block, block)
        agg_ref[:, pl.ds(at, block)] = jnp.dot(
            pooled_ref[...], w_ref[:, pl.ds(width + at, block)], preferred_element_type=F32
        ).astype(BF)

    total_ref[...] = out_ref[me].astype(F32)

    @pl.loop(1, total)
    def _(n):
        to = peer(n)
        at = to["tok"] * n_var + to["var"]
        copy = remote(out_ref.at[at], in_ref.at[at], sum_send.at[at], sum_recv.at[at], **to)
        copy.wait()
        total_ref[...] += in_ref[at].astype(F32)

    for c in range(chunks):
        sum_ref[:, c * lanes : (c + 1) * lanes] = total_ref[
            c * local_slots : (c + 1) * local_slots, :
        ]

    for copy in pat_copies:
        copy.wait_send()

    @pl.loop(1, n_tok)
    def _(n):
        wq_copy(n).wait_send()
        tok_copy(n).wait_send()
        for m in range(1, pairs):
            row_copy(n, m).wait_send()
        for m in range(pairs):
            sib_copy(n, m).wait_send()


def compute(n_tok, n_var, pat, slot, query, kw, vw, ow, pw, ve, cot):
    toks, width = cot.shape
    vars_ = ve.shape[0]
    rows = vw.shape[0]
    local_slots = slot.shape[1] // n_var
    pairs = n_var // 2
    total = n_tok * n_var
    chunks = 4 * width // n_tok // 128
    tall_out = -(-chunks * local_slots // 16) * 16
    vm = pl.BlockSpec(memory_space=pltpu.VMEM)
    dma = pltpu.SemaphoreType.DMA
    return pl.pallas_call(
        functools.partial(all_kernel, n_tok, n_var),
        out_shape=(
            jax.ShapeDtypeStruct((toks, width), BF),
            jax.ShapeDtypeStruct((local_slots, chunks * 128), F32),
        ),
        in_specs=[vm] * 9,
        out_specs=(vm, vm),
        scratch_shapes=[
            pltpu.VMEM((tall_out, 128), F32),
            pltpu.VMEM(pat.shape, BF),
            pltpu.VMEM((H, rows), F32),
            pltpu.VMEM((n_tok, H, rows), F32),
            pltpu.VMEM((width, 2 * width), BF),
            pltpu.VMEM((toks, vars_, 4), F32),
            pltpu.VMEM((toks, vars_, width), BF),
            pltpu.VMEM((toks, vars_, width), F32),
            pltpu.VMEM((width // 128 * H * toks, 128), F32),
            pltpu.VMEM((toks, vars_, H), F32),
            pltpu.VMEM((toks, vars_, H), F32),
            pltpu.VMEM((2 * H, width), BF),
            pltpu.VMEM((toks, width), BF),
            pltpu.VMEM((toks, vars_, 2 * H), BF),
            pltpu.VMEM((width // 128 * H * toks, 128), F32),
            pltpu.VMEM((4, vars_, width), F32),
            pltpu.VMEM((total, tall_out, 128), BF),
            pltpu.VMEM((total, tall_out, 128), BF),
            dma((n_var,)),
            dma((n_var,)),
            dma((n_tok,)),
            dma((n_tok,)),
            dma((n_tok,)),
            dma((n_tok,)),
            dma((n_tok * pairs,)),
            dma((n_tok * pairs,)),
            dma((n_tok * pairs,)),
            dma((n_tok * pairs,)),
            dma((total,)),
            dma((total,)),
        ],
        compiler_params=pltpu.CompilerParams(
            vmem_limit_bytes=56 * 1024 * 1024, collective_id=0, has_side_effects=True
        ),
    )(pat, slot, query, kw, vw, ow, pw, ve, cot)


def body(
    n_tok,
    n_var,
    patches,
    slot_var,
    patch_weight,
    var_embed,
    query,
    key_weight,
    value_weight,
    out_weight,
    cotangent,
):
    local_slots = patches.shape[0]
    toks = cotangent.shape[0]
    mine = patches.reshape(local_slots, 4, n_var, toks).transpose(2, 0, 1, 3)
    mine = mine.reshape(n_var, local_slots, 4 * toks)
    mine = jnp.pad(mine, ((0, 0), (0, -local_slots % 16), (0, 0)))
    return compute(
        n_tok,
        n_var,
        mine,
        slot_var.reshape(1, -1),
        query.reshape(1, -1),
        key_weight,
        value_weight,
        out_weight,
        patch_weight.transpose(1, 0, 2).astype(F32),
        var_embed,
        cotangent,
    )


def solution(mesh):
    return jax.shard_map(
        functools.partial(body, mesh.shape["tok"], mesh.shape["var"]),
        mesh=mesh,
        in_specs=(
            P("var", None, "tok"),
            P(),
            P(),
            P(),
            P(),
            P("tok", None),
            P("tok", None),
            P("tok", None),
            P(("tok", "var"), None),
        ),
        out_specs=(P(("tok", "var"), None), P("var", "tok")),
        check_vma=False,
    )
```
